1024 devices in a mesh: row: 32 (over x, y_lo, core), col: 32 (over y_hi, z).
Axes of the slice: x: 8, y: 8 (y_hi: 4, y_lo: 2; y = y_hi * 2 + y_lo), z: 8, core: 2. Of those that a mesh axis runs over, the one named last changes fastest.
Arguments:
- x_block: float32 [8, 262144], P(None, ('row', 'col')), may hold values from -45 to 45
- hx_block: float32 [8, 262144], P(None, ('row', 'col')), may hold values from -120 to 120
- p_block: float32 [8, 262144], P(None, ('row', 'col')), may hold values from -6 to 6
- hp_block: float32 [8, 262144], P(None, ('row', 'col')), may hold values from -6 to 6
- tile_values: bfloat16 [8192, 256, 256], P(('row', 'col')), may hold values from -0.125 to 0.125
- tile_rows: int32 [8192], P(('row', 'col')), may hold values from 0 to 31, as said below
- tile_cols: int32 [8192], P(('row', 'col')), may hold values from 0 to 31, as said below
- tile_count: int32 [1024], P(('row', 'col')), may hold values from 1 to 8, as said below
- coeffs: float32 [24, 8], replicated, may hold values from -3 to 3
Outputs:
- gram_h: float32 [24, 24], replicated
- gram_s: float32 [24, 24], replicated
- x_next: float32 [8, 262144], P(None, ('row', 'col'))
- hx_next: float32 [8, 262144], P(None, ('row', 'col'))
The draws below stay inside these ranges and needn't reach their ends.
Inputs may be any that keep to these rules, and one draw needn't show every extreme that they name: `tile_rows`: local tile row within the 32 tile rows of the device's grid row; the tile lies on or below the global diagonal. `tile_cols`: local tile column within the 32 tile columns of the device's grid column. `tile_count`: some device of the last grid row holds 8 live slots.
All inputs are finite; a program needn't handle non-finite values.
Results may differ from the reference program's by a relative error of at most 0.0012.
Values may be sent and summed in bfloat16 or wider, within the bound.
A program may use at most 32 MiB of HBM per device.

```python
import jax
import jax.numpy as jnp
from jax import lax

TILE = 256
STATES = 8
SPD = 1
TPD = 8
N = 262144
N_ROW = 32
N_COL = 32
DEVICES = 1024


def shared_fields(key, power):
    first_key, second_key, third_key = jax.random.split(key, 3)
    first = jnp.clip(jax.random.normal(first_key, (STATES, N), jnp.float32), -5.0, 5.0)
    second = jnp.clip(jax.random.normal(second_key, (STATES, N), jnp.float32), -5.0, 5.0)
    levels = jax.random.uniform(third_key, (STATES, 1), jnp.float32, -2.0, 2.0)
    place = jnp.arange(N, dtype=jnp.float32) / (N - 1)
    rising = (1.0 + 2.0 * place) ** power
    return (first * rising[None, :], (levels * first + 0.6 * second) * rising[None, :])


def draw_x_block(key, part):
    fields = shared_fields(key, 1.0)
    return fields[0]


def draw_hx_block(key, part):
    fields = shared_fields(key, 1.0)
    return fields[1]


def tile_pattern(key):
    col_key, row_key = jax.random.split(key)
    slot_ids = jnp.arange(DEVICES * TPD, dtype=jnp.int32)
    device_ids = slot_ids // TPD
    grid_row = device_ids // N_COL
    grid_col = device_ids % N_COL
    cols = jax.random.randint(col_key, (DEVICES * TPD,), 0, (grid_row + 1) * SPD, jnp.int32)
    floor = jnp.where(cols // SPD == grid_row, grid_col * SPD + cols % SPD, 0)
    rows = jax.random.randint(row_key, (DEVICES * TPD,), floor, N_COL * SPD, jnp.int32)
    return (rows, cols)


def draw_tile_rows(key, part):
    return tile_pattern(key)[0]


def draw_tile_cols(key, part):
    return tile_pattern(key)[1]


def draw_tile_count(key, part):
    key = jax.random.fold_in(key, 7)
    jitter_key, pick_key = jax.random.split(key)
    device_ids = jnp.arange(DEVICES, dtype=jnp.int32)
    grid_row = device_ids // N_COL
    base = jnp.maximum(TPD * (grid_row + 1) // N_ROW, TPD // 4)
    jitter = jax.random.randint(jitter_key, (DEVICES,), 0, TPD // 4 + 1, jnp.int32)
    counts = jnp.clip(base - jitter, 1, TPD)
    chosen = (N_ROW - 1) * N_COL + jax.random.randint(pick_key, (), 0, N_COL, jnp.int32)
    return jnp.where(device_ids == chosen, TPD, counts).astype(jnp.int32)


def block_scale(own_key, extent, shards, low, largest):
    def one(axis_at, parts):
        draws = jax.random.uniform(jax.random.fold_in(jax.random.fold_in(own_key, 6), axis_at), (parts,), jnp.float32, low / len(shards), largest / len(shards))
        return jnp.repeat(jnp.exp(draws), extent[axis_at] // parts).reshape((-1,) + (1,) * (len(extent) - axis_at - 1))

    gain = one(*shards[0])
    for cut in shards[1:]:
        gain = gain * one(*cut)
    return gain


def gaussian(rng, shape, deviation, bound, cuts=(), kind=jnp.bfloat16):
    values = jax.random.normal(rng, shape, jnp.float32) * deviation
    if len(cuts) > 0:
        values = block_scale(rng, shape, cuts, -0.22, 0.18) * values
    return jnp.clip(values, min=-bound, max=bound).astype(kind)


def setup_inputs(seed: int = 0) -> dict:
    splits = jax.random.split(jax.random.key(seed), 10)
    x_block = draw_x_block(jax.random.fold_in(splits[9], 71), 0)
    hx_block = draw_hx_block(jax.random.fold_in(splits[9], 71), 0)
    p_block = gaussian(splits[2], (STATES, N), 1.0, 6.0, ((1, 1024),), jnp.float32)
    hp_block = gaussian(splits[3], (STATES, N), 1.5, 6.0, ((1, 1024),), jnp.float32)
    tile_values = gaussian(splits[4], (DEVICES * TPD, TILE, TILE), (TILE * TPD) ** -0.5, 0.125, ((0, 1024),))
    tile_rows = draw_tile_rows(jax.random.fold_in(splits[9], 71), 0)
    tile_cols = draw_tile_cols(jax.random.fold_in(splits[9], 71), 0)
    tile_count = draw_tile_count(jax.random.fold_in(splits[9], 71), 0)
    coeffs = gaussian(splits[8], (3 * STATES, STATES), 0.5, 3.0, (), jnp.float32)
    return dict(x_block=x_block, hx_block=hx_block, p_block=p_block, hp_block=hp_block, tile_values=tile_values, tile_rows=tile_rows, tile_cols=tile_cols, tile_count=tile_count, coeffs=coeffs)


def reference(x_block, hx_block, p_block, hp_block, tile_values, tile_rows, tile_cols, tile_count, coeffs):
    highest = lax.Precision.HIGHEST
    theta_vals = jnp.sum(x_block * hx_block, axis=1) / jnp.sum(x_block * x_block, axis=1)
    residual = hx_block - theta_vals[:, None] * x_block
    resid_half = residual.astype(jnp.bfloat16)
    tile_total = N // TILE
    vec_tiles = resid_half.astype(jnp.float32).reshape(STATES, tile_total, TILE).transpose(1, 0, 2)
    slot_ids = jnp.arange(DEVICES * TPD, dtype=jnp.int32)
    device_ids = (slot_ids // TPD).astype(jnp.int32)
    grid_row = device_ids // N_COL
    grid_col = device_ids % N_COL
    global_rows = (grid_row * N_COL * SPD + tile_rows).astype(jnp.int32)
    global_cols = (((tile_cols // SPD) * N_COL + grid_col) * SPD + tile_cols % SPD).astype(jnp.int32)
    live_mask = ((slot_ids % TPD) < tile_count[device_ids]).astype(jnp.float32)
    picked_cols = vec_tiles[global_cols]
    picked_rows = vec_tiles[global_rows]

    def device_terms(pieces):
        tile_block, by_cols, by_rows = pieces
        block = tile_block.astype(jnp.float32)
        return (jnp.einsum("sij,skj->ski", block, by_cols), jnp.einsum("sij,ski->skj", block, by_rows))

    forward, mirror = lax.map(device_terms, (tile_values.reshape(DEVICES, TPD, TILE, TILE),
                                             picked_cols.reshape(DEVICES, TPD, STATES, TILE),
                                             picked_rows.reshape(DEVICES, TPD, STATES, TILE)))
    forward = forward.reshape(DEVICES * TPD, STATES, TILE) * live_mask[:, None, None]
    mirror = mirror.reshape(DEVICES * TPD, STATES, TILE) * live_mask[:, None, None]
    image_tiles = jax.ops.segment_sum(forward, global_rows, num_segments=tile_total)
    image_tiles = image_tiles + jax.ops.segment_sum(mirror, global_cols, num_segments=tile_total)
    image = image_tiles.transpose(1, 0, 2).reshape(STATES, N)
    basis = jnp.concatenate([x_block, residual, p_block], axis=0)
    basis_image = jnp.concatenate([hx_block, image, hp_block], axis=0)
    gram_h = jnp.dot(basis, basis_image.T, precision=highest) / N
    gram_s = jnp.dot(basis, basis.T, precision=highest) / N
    x_next = jnp.dot(coeffs.T, basis, precision=highest)
    hx_next = jnp.dot(coeffs.T, basis_image, precision=highest)
    return gram_h, gram_s, x_next, hx_next
```

```python
import functools

import jax
import jax.numpy as jnp
from jax import lax
from jax.experimental import pallas as pl
from jax.experimental.pallas import tpu as pltpu
from jax.sharding import PartitionSpec as P

MESH = pl.DeviceIdType.MESH
F32 = jnp.float32
BF16 = jnp.bfloat16
EXACT = lax.Precision.HIGHEST
LEVELS = 32767.0
NT = (((1,), (1,)), ((), ()))
NN = (((1,), (0,)), ((), ()))
TN = (((0,), (0,)), ((), ()))


def iota(shape, axis):
    return lax.broadcasted_iota(jnp.int32, shape, axis)


def dot(a, b, dims, precision=None):
    return lax.dot_general(a, b, dims, precision=precision, preferred_element_type=F32)


def to_row(columns):
    lane, sub = iota((8, 128), 1), iota((8, 128), 0)
    total = jnp.zeros((8, 128), F32)
    for place, column in enumerate(columns):
        total = total + jnp.where(lane == sub + 8 * place, column, 0.0)
    return jnp.sum(total, axis=0, keepdims=True)


def from_row(row, place):
    lane, sub = iota((8, 128), 1), iota((8, 128), 0)
    return jnp.sum(jnp.where(lane == sub + 8 * place, row, 0.0), axis=1, keepdims=True)


def halves(v):
    return v[:, :128], v[:, 128:]


def coded(v):
    top = jnp.max(jnp.abs(v), axis=1, keepdims=True)
    usable = top > 1e-30
    inverse = jnp.where(usable, LEVELS / jnp.where(usable, top, 1.0), 0.0)
    return jnp.round(v * inverse), top * (1.0 / LEVELS)


def split(v):
    high = v.astype(BF16)
    return high, (v - high.astype(F32)).astype(BF16)


def wait(ref, sem):
    pltpu.make_async_copy(ref, ref, sem).wait()


def kernel(
    rows_n, cols_n, cells, slots,
    x_ref, hx_ref, p_ref, hp_ref, tiles_hbm, rows_ref, cols_ref, count_ref, coef_ref,
    xn_ref, hxn_ref, gh_ref, gs_ref,
    tiles, stat, rstat, cstat, csum, csums, bundle, rbun, cbun,
    early, erow, esum, ecol, late, lrow, lsum, lcol, rsend, csend, rrecv, crecv,
    tile_sem, send, recv,
):
    r, c = lax.axis_index("row"), lax.axis_index("col")

    def along_col(i):
        return lax.rem(c + 1 + i, cols_n)

    def along_row(i):
        return lax.rem(r + 1 + i, rows_n)

    def each(n, f):
        def step(i, carry):
            f(i)
            return carry
        lax.fori_loop(0, n - 1, step, 0)

    def push(src, dst, k, axis, j):
        pltpu.make_async_remote_copy(
            src_ref=src, dst_ref=dst, send_sem=send.at[k], recv_sem=recv.at[k],
            device_id={axis: j}, device_id_type=MESH,
        ).start()

    barrier = pltpu.get_barrier_semaphore()
    each(cols_n, lambda i: pl.semaphore_signal(
        barrier, inc=1, device_id={"col": along_col(i)}, device_id_type=MESH))
    each(rows_n, lambda i: pl.semaphore_signal(
        barrier, inc=1, device_id={"row": along_row(i)}, device_id_type=MESH))
    tile_copy = pltpu.make_async_copy(tiles_hbm, tiles, tile_sem)
    tile_copy.start()

    x, hx, p, hp = x_ref[...], hx_ref[...], p_ref[...], hp_ref[...]
    cross = jnp.sum(x * hx, axis=1, keepdims=True)
    square = jnp.sum(x * x, axis=1, keepdims=True)
    some = square > 0.0
    guess = jnp.where(some, cross / jnp.where(some, square, 1.0), 0.0)
    near = hx - guess * x
    near_code, near_step = coded(near)
    x_code, x_step = coded(x)
    p_code, p_step = coded(p)
    row = to_row([cross, square, guess, near_step, x_step, p_step])
    stat[...] = row
    rstat[c] = row
    cstat[r] = row
    (nl, nh), (xl, xh), (pl_, ph) = halves(near_code), halves(x_code), halves(p_code)
    packed = jnp.concatenate([nl, xl, nh, xh, pl_, ph], axis=0).astype(jnp.int32).astype(jnp.int16)
    bundle[...] = packed
    rbun[c] = packed
    cbun[r] = packed

    pl.semaphore_wait(barrier, rows_n + cols_n - 2)

    each(cols_n, lambda i: push(stat, rstat.at[c], 0, "col", along_col(i)))
    each(rows_n, lambda i: push(stat, cstat.at[r], 1, "row", along_row(i)))

    def push_bundle(i):
        push(bundle, rbun.at[c], 2, "col", along_col(i))
        push(bundle, cbun.at[r], 3, "row", along_row(i))

    if rows_n == cols_n:
        each(cols_n, push_bundle)

    lane, sub = iota((8, 128), 1), iota((8, 128), 0)
    own_state = lax.rem(lane, 8) == sub
    slot_of = lax.rem(lane, 8 * slots) // 8

    def onehot(ids, n):
        place = jnp.zeros((8, 128), jnp.int32)
        for s in range(slots):
            place = jnp.where(slot_of == s, ids[s], place)
        blocks = [jnp.where((place == d) & own_state, 1.0, 0.0) for d in range(n)]
        return jnp.concatenate(blocks, axis=0).astype(BF16)

    row_hot, col_hot = onehot(rows_ref, cols_n), onehot(cols_ref, rows_n)

    wait(rstat.at[pl.ds(0, cols_n - 1)], recv.at[0])
    col_total = jnp.sum(rstat[...], axis=0)
    csum[...] = col_total
    csums[r] = col_total
    each(rows_n, lambda i: push(csum, csums.at[r], 4, "row", along_row(i)))
    wait(csums.at[pl.ds(0, rows_n - 1)], recv.at[4])
    total = jnp.sum(csums[...], axis=0)
    theta = from_row(total, 0) / from_row(total, 1)
    residual = hx - theta * x

    basis = jnp.concatenate([x, residual, p], axis=0)
    others = jnp.concatenate([basis, hx, hp, jnp.zeros((88, x.shape[1]), F32)], axis=0)
    products = dot(basis, others, NT, EXACT)
    tile = (products[0:8] + pltpu.roll(products[8:16], 40, 1)) + pltpu.roll(products[16:24], 80, 1)
    early[...] = tile
    erow[r] = tile
    each(rows_n, lambda i: push(early, erow.at[r], 5, "row", along_row(i)))

    wait(rbun.at[pl.ds(0, cols_n - 1)], recv.at[2])
    wait(cbun.at[pl.ds(0, rows_n - 1)], recv.at[3])
    wait(cstat.at[pl.ds(0, rows_n - 1)], recv.at[1])
    tile_copy.wait()

    def fetch(stats, shards, at):
        numbers = stats[at]
        code = shards[at].astype(jnp.int32).astype(F32)
        near_part = from_row(numbers, 3)
        x_part = from_row(numbers, 4)
        p_part = from_row(numbers, 5)
        shift = (from_row(numbers, 2) - theta) * x_part
        wide = lambda a, b: jnp.concatenate([code[a:a + 8], code[b:b + 8]], axis=1)
        x_wide = wide(8, 24)
        res = near_part * wide(0, 16) + shift * x_wide
        return res, jnp.concatenate([x_part * x_wide, res, p_part * wide(32, 40)], axis=0)

    forward, mirror = [], []
    partial = jnp.zeros((16, 48), F32)
    for s in range(slots):
        live = jnp.where(s < count_ref[0], 1.0, 0.0).astype(F32)
        by_col, col_basis = fetch(cstat, cbun, cols_ref[s])
        by_row, row_basis = fetch(rstat, rbun, rows_ref[s])
        matrix = tiles[s]
        f = dot(by_col.astype(BF16), matrix, NT) * live
        m = dot(by_row.astype(BF16), matrix, NN) * live
        fh, fl = split(f)
        mh, ml = split(m)
        forward.append((fh, fl))
        mirror.append((mh, ml))
        rb = jnp.concatenate(split(row_basis), axis=0)
        cb = jnp.concatenate(split(col_basis), axis=0)
        partial = partial + dot(jnp.concatenate([fh, fl], axis=0), rb, NT)
        partial = partial + dot(jnp.concatenate([mh, ml], axis=0), cb, NT)

    g = partial[0:8] + partial[8:16]
    from_lane = iota((48, 256), 0)
    to_lane = lax.rem(iota((48, 256), 1), 32)
    spread = jnp.where((from_lane == to_lane) & (to_lane < 24) | (from_lane == to_lane + 24) & (to_lane < 24), 1.0, 0.0)
    g = dot(g, spread, NN, EXACT)
    g = jnp.sum(jnp.where(iota((8, 256), 1) // 32 == iota((8, 256), 0), g, 0.0), axis=0, keepdims=True)
    flat = jnp.concatenate([g[:, :128], g[:, 128:]], axis=0)
    late[...] = flat
    lrow[r] = flat
    each(rows_n, lambda i: push(late, lrow.at[r], 7, "row", along_row(i)))

    def spread_out(hot, parts, n, buffer):
        stack = jnp.concatenate([h for h, _ in parts] + [l for _, l in parts], axis=0)
        out = dot(hot, stack, NN)
        left, right = halves(out)
        out = jnp.concatenate([left.reshape(n, 8, 128), right.reshape(n, 8, 128)], axis=1)
        buffer[...] = out.astype(BF16)

    spread_out(row_hot, forward, cols_n, rsend)
    spread_out(col_hot, mirror, rows_n, csend)

    def push_parts(i):
        j, k = along_col(i), along_row(i)
        push(rsend.at[j], rrecv.at[c], 9, "col", j)
        push(csend.at[k], crecv.at[r], 10, "row", k)

    if rows_n == cols_n:
        each(cols_n, push_parts)
    rrecv[c] = rsend[c]
    crecv[r] = csend[r]

    wait(erow.at[pl.ds(0, rows_n - 1)], recv.at[5])
    tile = jnp.sum(erow[...], axis=0)
    esum[...] = tile
    ecol[c] = tile
    each(cols_n, lambda i: push(esum, ecol.at[c], 6, "col", along_col(i)))

    wait(lrow.at[pl.ds(0, rows_n - 1)], recv.at[7])
    flat = jnp.sum(lrow[...], axis=0)
    lsum[...] = flat
    lcol[c] = flat
    each(cols_n, lambda i: push(lsum, lcol.at[c], 8, "col", along_col(i)))

    coef = coef_ref[...]
    xn_ref[...] = dot(coef, basis, TN, EXACT)

    wait(rrecv.at[pl.ds(0, cols_n - 1)], recv.at[9])
    wait(crecv.at[pl.ds(0, rows_n - 1)], recv.at[10])
    image = jnp.sum(rrecv[...].astype(F32), axis=0) + jnp.sum(crecv[...].astype(F32), axis=0)
    image = jnp.concatenate([image[0:8], image[8:16]], axis=1)
    hxn_ref[...] = dot(coef, jnp.concatenate([hx, image, hp], axis=0), TN, EXACT)

    scale = 1.0 / cells
    wait(ecol.at[pl.ds(0, cols_n - 1)], recv.at[6])
    tile = jnp.sum(ecol[...], axis=0)
    products = jnp.concatenate([tile, pltpu.roll(tile, 88, 1), pltpu.roll(tile, 48, 1)], axis=0) * scale
    gs_ref[...] = products[:, :24]

    wait(lcol.at[pl.ds(0, cols_n - 1)], recv.at[8])
    flat = jnp.sum(lcol[...], axis=0)
    flat = jnp.concatenate([flat[0:1], flat[1:2]], axis=1)
    mine = lax.rem(iota((24, 256), 1), 32) == iota((24, 256), 0)
    gather = jnp.where(iota((256, 128), 1) == 8 + iota((256, 128), 0) // 32, scale, 0.0)
    middle = dot(jnp.where(mine, flat, 0.0), gather, NN, EXACT)
    at = iota((24, 128), 1)
    full = jnp.where(at < 8, pltpu.roll(products, 104, 1), jnp.where(at < 16, middle, pltpu.roll(products, 112, 1)))
    gh_ref[...] = full[:, :24]

    for k, ref, n in ((0, rstat, cols_n), (1, cstat, rows_n), (2, rbun, cols_n), (3, cbun, rows_n),
                      (4, csums, rows_n), (5, erow, rows_n), (6, ecol, cols_n), (7, lrow, rows_n),
                      (8, lcol, cols_n), (9, rrecv, cols_n), (10, crecv, rows_n)):
        wait(ref.at[pl.ds(0, n - 1)], send.at[k])


def body(x_block, hx_block, p_block, hp_block, tile_values, tile_rows, tile_cols, tile_count, coeffs):
    rows_n, cols_n = lax.axis_size("row"), lax.axis_size("col")
    states, length = x_block.shape
    slots = tile_values.shape[0]
    vmem = pl.BlockSpec(memory_space=pltpu.VMEM)
    smem = pl.BlockSpec(memory_space=pltpu.SMEM)
    small, big, word = pltpu.VMEM, pltpu.VMEM, jnp.int16
    gh, gs, xn, hxn = (2, 3, 0, 1)
    outs = pl.pallas_call(
        functools.partial(kernel, rows_n, cols_n, length * rows_n * cols_n, slots),
        out_shape=(
            jax.ShapeDtypeStruct((states, length), F32),
            jax.ShapeDtypeStruct((states, length), F32),
            jax.ShapeDtypeStruct((24, 24), F32),
            jax.ShapeDtypeStruct((24, 24), F32),
        ),
        in_specs=[vmem] * 4 + [pl.BlockSpec(memory_space=pltpu.HBM)] + [smem] * 3 + [vmem],
        out_specs=(vmem,) * 4,
        scratch_shapes=[
            pltpu.VMEM(tile_values.shape, BF16),
            pltpu.VMEM((1, 128), F32),
            pltpu.VMEM((cols_n, 1, 128), F32),
            pltpu.VMEM((rows_n, 1, 128), F32),
            pltpu.VMEM((1, 128), F32),
            pltpu.VMEM((rows_n, 1, 128), F32),
            pltpu.VMEM((48, 128), word),
            pltpu.VMEM((cols_n, 48, 128), word),
            pltpu.VMEM((rows_n, 48, 128), word),
            pltpu.VMEM((8, 128), F32),
            pltpu.VMEM((rows_n, 8, 128), F32),
            pltpu.VMEM((8, 128), F32),
            pltpu.VMEM((cols_n, 8, 128), F32),
            pltpu.VMEM((2, 128), F32),
            pltpu.VMEM((rows_n, 2, 128), F32),
            pltpu.VMEM((2, 128), F32),
            pltpu.VMEM((cols_n, 2, 128), F32),
            pltpu.VMEM((cols_n, 16, 128), BF16),
            pltpu.VMEM((rows_n, 16, 128), BF16),
            pltpu.VMEM((cols_n, 16, 128), BF16),
            pltpu.VMEM((rows_n, 16, 128), BF16),
            pltpu.SemaphoreType.DMA,
            pltpu.SemaphoreType.DMA((11,)),
            pltpu.SemaphoreType.DMA((11,)),
        ],
        compiler_params=pltpu.CompilerParams(
            collective_id=0, has_side_effects=True, vmem_limit_bytes=32 << 20
        ),
        name="step",
    )(x_block, hx_block, p_block, hp_block, tile_values, tile_rows, tile_cols, tile_count, coeffs)
    return outs[gh], outs[gs], outs[xn], outs[hxn]


def solution(mesh):
    both = ("row", "col")
    return jax.shard_map(
        body,
        mesh=mesh,
        in_specs=(
            P(None, both), P(None, both), P(None, both), P(None, both),
            P(both, None, None), P(both), P(both), P(both), P(),
        ),
        out_specs=(P(), P(), P(None, both), P(None, both)),
        check_vma=False,
    )
```

```python
import functools

import jax
import jax.numpy as jnp
from jax import lax
from jax.experimental import pallas as pl
from jax.experimental.pallas import tpu as pltpu
from jax.sharding import PartitionSpec as P

MESH = pl.DeviceIdType.MESH
F32 = jnp.float32
BF16 = jnp.bfloat16
EXACT = lax.Precision.HIGHEST
LEVELS = 32767.0
LIMIT = 60 << 20
NT = (((1,), (1,)), ((), ()))
NN = (((1,), (0,)), ((), ()))


def iota(shape, axis):
    return lax.broadcasted_iota(jnp.int32, shape, axis)


def dot(a, b, dims, precision=None):
    return lax.dot_general(a, b, dims, precision=precision, preferred_element_type=F32)


def to_row(columns):
    lane, sub = iota((8, 128), 1), iota((8, 128), 0)
    total = jnp.zeros((8, 128), F32)
    for place, column in enumerate(columns):
        total = total + jnp.where(lane == sub + 8 * place, column, 0.0)
    return jnp.sum(total, axis=0, keepdims=True)


def from_row(row, place):
    lane, sub = iota((8, 128), 1), iota((8, 128), 0)
    return jnp.sum(jnp.where(lane == sub + 8 * place, row, 0.0), axis=1, keepdims=True)


def halves(v):
    return v[:, :128], v[:, 128:]


def coded(v):
    top = jnp.max(jnp.abs(v), axis=1, keepdims=True)
    usable = top > 1e-30
    inverse = jnp.where(usable, LEVELS / jnp.where(usable, top, 1.0), 0.0)
    return jnp.round(v * inverse), top * (1.0 / LEVELS)


def split(v):
    high = v.astype(BF16)
    return high, (v - high.astype(F32)).astype(BF16)


def wait(ref, sem):
    pltpu.make_async_copy(ref, ref, sem).wait()


def near_of(n):
    return 4 if n >= 16 else 2


def kernel(
    rows_n, cols_n, cells, slots,
    x_hbm, hx_hbm, p_hbm, hp_hbm, tiles_hbm, rows_hbm, cols_hbm, count_hbm, coef_hbm,
    xn_ref, hxn_ref, gh_ref, gs_ref,
    x_ref, hx_ref, p_ref, hp_ref, tiles, rows_ref, cols_ref, count_ref, coef_ref,
    stat, rstat, cstat, csum, csums, near_send, rnear, cnear, pair_send, rpair, cpair,
    early, early_x, early_q, early_h, early_z, late, lrow, lsum, lcol, rsend, csend, rrecv, crecv,
    load, send, recv,
):
    r, c = lax.axis_index("row"), lax.axis_index("col")
    near_n, high_n = near_of(rows_n), near_of(cols_n)
    x_n, z_n = rows_n // near_n, cols_n // high_n
    my_x, my_q = r // near_n, lax.rem(r, near_n)
    my_h, my_z = c // z_n, lax.rem(c, z_n)
    my_slot = my_z * high_n + my_h
    my_near = my_q * x_n + my_x

    def along_col(i):
        return lax.rem(c + 1 + i, cols_n)

    def along_row(i):
        return lax.rem(r + 1 + i, rows_n)

    def each(n, f):
        def step(i, carry):
            f(i)
            return carry
        lax.fori_loop(0, n - 1, step, 0)

    def push(src, dst, k, axis, j):
        pltpu.make_async_remote_copy(
            src_ref=src, dst_ref=dst, send_sem=send.at[k], recv_sem=recv.at[k],
            device_id={axis: j}, device_id_type=MESH,
        ).start()

    table = (
        (0, rstat, cols_n - 1), (1, cstat, rows_n - 1), (4, csums, rows_n - 1),
        (5, cpair, near_n - 1), (13, cpair, rows_n - near_n), (6, rpair, high_n - 1), (14, rpair, cols_n - high_n),
        (3, cnear, x_n - 1), (18, cnear, rows_n - x_n), (2, rnear, z_n - 1), (17, rnear, cols_n - z_n),
        (16, early_z, z_n - 1), (15, early_h, high_n - 1), (11, early_x, x_n - 1), (12, early_q, near_n - 1),
        (7, lrow, rows_n - 1), (8, lcol, cols_n - 1), (9, rrecv, cols_n - 1), (10, crecv, rows_n - 1),
    )

    def arrive(k):
        ref, n = next((ref, n) for j, ref, n in table if j == k)
        wait(ref.at[pl.ds(0, n)], recv.at[k])

    loads = [
        pltpu.make_async_copy(a, b, load.at[k])
        for k, (a, b) in enumerate((
            (x_hbm, x_ref), (hx_hbm, hx_ref), (p_hbm, p_ref), (hp_hbm, hp_ref), (tiles_hbm, tiles),
            (rows_hbm, rows_ref), (cols_hbm, cols_ref), (count_hbm, count_ref), (coef_hbm, coef_ref)))
    ]
    for copy in loads:
        copy.start()
    barrier = pltpu.get_barrier_semaphore()
    each(cols_n, lambda i: pl.semaphore_signal(
        barrier, inc=1, device_id={"col": along_col(i)}, device_id_type=MESH))
    each(rows_n, lambda i: pl.semaphore_signal(
        barrier, inc=1, device_id={"row": along_row(i)}, device_id_type=MESH))
    for k in (0, 1, 2, 3, 5, 6, 7, 8):
        loads[k].wait()

    x, hx, p, hp = x_ref[...], hx_ref[...], p_ref[...], hp_ref[...]
    cross = jnp.sum(x * hx, axis=1, keepdims=True)
    square = jnp.sum(x * x, axis=1, keepdims=True)
    some = square > 0.0
    guess = jnp.where(some, cross / jnp.where(some, square, 1.0), 0.0)
    near = hx - guess * x
    near_code, near_step = coded(near)
    x_code, x_step = coded(x)
    p_code, p_step = coded(p)
    row = to_row([cross, square, guess, near_step, x_step, p_step])
    stat[...] = row
    rstat[c] = row
    cstat[r] = row
    near_code = jnp.concatenate(halves(near_code), axis=0).astype(jnp.int32).astype(jnp.int16)
    near_send[...] = near_code
    rnear[c] = near_code
    cnear[my_near] = near_code
    pair = jnp.concatenate(halves(x_code) + halves(p_code), axis=0).astype(jnp.int32).astype(jnp.int16)
    pair_send[...] = pair
    rpair[my_slot] = pair
    cpair[r] = pair

    pl.semaphore_wait(barrier, rows_n + cols_n - 2)

    def offsets(n, f):
        for i in range(1, n):
            f(i)

    def at_x(i):
        return lax.rem(my_x + i, x_n) * near_n + my_q

    def at_q(i):
        return my_x * near_n + lax.rem(my_q + i, near_n)

    def at_z(i):
        return my_h * z_n + lax.rem(my_z + i, z_n)

    def at_h(i):
        return lax.rem(my_h + i, high_n) * z_n + my_z

    each(cols_n, lambda i: push(stat, rstat.at[c], 0, "col", along_col(i)))
    offsets(high_n, lambda i: push(pair_send, rpair.at[my_slot], 6, "col", at_h(i)))
    offsets(near_n, lambda i: push(pair_send, cpair.at[r], 5, "row", at_q(i)))
    offsets(z_n, lambda i: push(near_send, rnear.at[c], 2, "col", at_z(i)))
    offsets(x_n, lambda i: push(near_send, cnear.at[my_near], 3, "row", at_x(i)))
    each(rows_n, lambda i: push(stat, cstat.at[r], 1, "row", along_row(i)))

    lane, sub = iota((8, 128), 1), iota((8, 128), 0)
    own_state = lax.rem(lane, 8) == sub
    slot_of = lax.rem(lane, 8 * slots) // 8

    def onehot(ids, n):
        place = jnp.zeros((8, 128), jnp.int32)
        for s in range(slots):
            place = jnp.where(slot_of == s, ids[s], place)
        blocks = [jnp.where((place == d) & own_state, 1.0, 0.0) for d in range(n)]
        return jnp.concatenate(blocks, axis=0).astype(BF16)

    row_hot, col_hot = onehot(rows_ref, cols_n), onehot(cols_ref, rows_n)

    def onward(n, ref, first, size, k, axis, at):
        group = ref.at[pl.ds(first, size)]
        offsets(n, lambda i: push(group, group, k, axis, at(i)))

    arrive(5)
    onward(x_n, cpair, my_x * near_n, near_n, 13, "row", at_x)
    arrive(3)
    onward(near_n, cnear, my_q * x_n, x_n, 18, "row", at_q)
    arrive(6)
    onward(z_n, rpair, my_z * high_n, high_n, 14, "col", at_z)
    arrive(2)
    onward(high_n, rnear, my_h * z_n, z_n, 17, "col", at_h)

    arrive(0)
    col_total = jnp.sum(rstat[...], axis=0)
    csum[...] = col_total
    csums[r] = col_total
    each(rows_n, lambda i: push(csum, csums.at[r], 4, "row", along_row(i)))
    row_cross, row_square = from_row(col_total, 0), from_row(col_total, 1)
    some = row_square > 0.0
    row_theta = jnp.where(some, row_cross / jnp.where(some, row_square, 1.0), 0.0)
    basis = jnp.concatenate([x, hx - row_theta * x, p], axis=0)
    others = jnp.concatenate([basis, hx, hp, jnp.zeros((88, x.shape[1]), F32)], axis=0)
    products = dot(basis, others, NT, EXACT)
    tile = (products[0:8] + pltpu.roll(products[8:16], 40, 1)) + pltpu.roll(products[16:24], 80, 1)
    early[0] = tile
    early_z[my_z] = tile
    offsets(z_n, lambda i: push(early.at[0], early_z.at[my_z], 16, "col", at_z(i)))

    arrive(1)

    def numbers(row):
        return [from_row(row, place) for place in (2, 3, 4, 5)]

    col_numbers = [numbers(cstat[cols_ref[s]]) for s in range(slots)]
    row_numbers = [numbers(rstat[rows_ref[s]]) for s in range(slots)]

    def early_step(k, n, gathered):
        arrive(k)
        return jnp.sum(gathered[...], axis=0)

    tile = early_step(16, z_n, early_z)
    early[1] = tile
    early_h[my_h] = tile
    offsets(high_n, lambda i: push(early.at[1], early_h.at[my_h], 15, "col", at_h(i)))

    arrive(4)
    total = jnp.sum(csums[...], axis=0)
    theta = from_row(total, 0) / from_row(total, 1)
    residual = hx - theta * x
    basis = jnp.concatenate([x, residual, p], axis=0)

    for k in (18, 17, 13, 14):
        arrive(k)
    loads[4].wait()

    def fetch(numbers, near_words, pair_words):
        guess, near_part, x_part, p_part = numbers
        near_code = near_words.astype(jnp.int32).astype(F32)
        pair_code = pair_words.astype(jnp.int32).astype(F32)
        x_wide = jnp.concatenate([pair_code[0:8], pair_code[8:16]], axis=1)
        p_wide = jnp.concatenate([pair_code[16:24], pair_code[24:32]], axis=1)
        near_wide = jnp.concatenate([near_code[0:8], near_code[8:16]], axis=1)
        res = near_part * near_wide + ((guess - theta) * x_part) * x_wide
        return res, jnp.concatenate([x_part * x_wide, res, p_part * p_wide], axis=0)

    forward, mirror, left, right = [], [], [], []
    for s in range(slots):
        live = jnp.where(s < count_ref[0], 1.0, 0.0).astype(F32)
        at_col, at_row = cols_ref[s], rows_ref[s]
        by_col, col_basis = fetch(
            col_numbers[s], cnear[lax.rem(at_col, near_n) * x_n + at_col // near_n], cpair[at_col])
        by_row, row_basis = fetch(
            row_numbers[s], rnear[at_row], rpair[lax.rem(at_row, z_n) * high_n + at_row // z_n])
        matrix = tiles[s]
        forward.append(split(dot(by_col.astype(BF16), matrix, NT) * live))
        mirror.append(split(dot(by_row.astype(BF16), matrix, NN) * live))
        left += [jnp.concatenate(forward[-1], axis=0), jnp.concatenate(mirror[-1], axis=0)]
        right += [jnp.concatenate(split(row_basis), axis=0), jnp.concatenate(split(col_basis), axis=0)]
    partial = dot(jnp.concatenate(left, axis=1), jnp.concatenate(right, axis=1), NT)

    g = partial[0:8] + partial[8:16]
    from_lane = iota((48, 256), 0)
    to_lane = lax.rem(iota((48, 256), 1), 32)
    spread = jnp.where((from_lane == to_lane) & (to_lane < 24) | (from_lane == to_lane + 24) & (to_lane < 24), 1.0, 0.0)
    g = dot(g, spread, NN, EXACT)
    g = jnp.sum(jnp.where(iota((8, 256), 1) // 32 == iota((8, 256), 0), g, 0.0), axis=0, keepdims=True)
    flat = jnp.concatenate([g[:, :128], g[:, 128:]], axis=0)
    late[...] = flat
    lrow[r] = flat
    each(rows_n, lambda i: push(late, lrow.at[r], 7, "row", along_row(i)))

    def spread_out(hot, parts, n, buffer):
        stack = jnp.concatenate([h for h, _ in parts] + [l for _, l in parts], axis=0)
        out = dot(hot, stack, NN)
        left, right = halves(out)
        out = jnp.concatenate([left.reshape(n, 8, 128), right.reshape(n, 8, 128)], axis=1)
        buffer[...] = out.astype(BF16)

    spread_out(row_hot, forward, cols_n, rsend)
    spread_out(col_hot, mirror, rows_n, csend)

    def push_parts(i):
        j, k = along_col(i), along_row(i)
        push(rsend.at[j], rrecv.at[c], 9, "col", j)
        push(csend.at[k], crecv.at[r], 10, "row", k)

    each(cols_n, push_parts)
    rrecv[c] = rsend[c]
    crecv[r] = csend[r]

    tile = early_step(15, high_n, early_h)
    shift = row_theta - theta
    in_rows = (lane >= 40) & (lane < 80)
    tile = tile + jnp.where(in_rows, shift * pltpu.roll(tile, 40, 1), 0.0)
    columns = jnp.where(lax.rem(lane, 40) == sub + 8, shift, 0.0)
    tile = tile + jnp.sum(columns, axis=0, keepdims=True) * pltpu.roll(tile, 8, 1)
    early[2] = tile
    early_x[my_x] = tile
    offsets(x_n, lambda i: push(early.at[2], early_x.at[my_x], 11, "row", at_x(i)))

    arrive(7)
    flat = jnp.sum(lrow[...], axis=0)
    lsum[...] = flat
    lcol[c] = flat
    each(cols_n, lambda i: push(lsum, lcol.at[c], 8, "col", along_col(i)))

    tile = early_step(11, x_n, early_x)
    early[3] = tile
    early_q[my_q] = tile
    offsets(near_n, lambda i: push(early.at[3], early_q.at[my_q], 12, "row", at_q(i)))

    coef = coef_ref[...]
    xn_ref[...] = dot(coef, basis, NN, EXACT)

    arrive(9)
    arrive(10)
    image = jnp.sum(rrecv[...].astype(F32), axis=0) + jnp.sum(crecv[...].astype(F32), axis=0)
    image = jnp.concatenate([image[0:8], image[8:16]], axis=1)
    hxn_ref[...] = dot(coef, jnp.concatenate([hx, image, hp], axis=0), NN, EXACT)

    scale = 1.0 / cells
    tile = early_step(12, near_n, early_q)
    products = jnp.concatenate([tile, pltpu.roll(tile, 88, 1), pltpu.roll(tile, 48, 1)], axis=0) * scale
    gs_ref[...] = products[:, :24]

    arrive(8)
    flat = jnp.sum(lcol[...], axis=0)
    flat = jnp.concatenate([flat[0:1], flat[1:2]], axis=1)
    mine = lax.rem(iota((24, 256), 1), 32) == iota((24, 256), 0)
    gather = jnp.where(iota((256, 128), 1) == 8 + iota((256, 128), 0) // 32, scale, 0.0)
    middle = dot(jnp.where(mine, flat, 0.0), gather, NN, EXACT)
    at = iota((24, 128), 1)
    full = jnp.where(at < 8, pltpu.roll(products, 104, 1), jnp.where(at < 16, middle, pltpu.roll(products, 112, 1)))
    gh_ref[...] = full[:, :24]

    for k, ref, n in table:
        wait(ref.at[pl.ds(0, n)], send.at[k])


def hand_over(xn_ref, hxn_ref, gh_ref, gs_ref, gh_out, gs_out, xn_out, hxn_out, sems):
    pairs = ((gh_ref, gh_out), (gs_ref, gs_out), (xn_ref, xn_out), (hxn_ref, hxn_out))
    copies = [pltpu.make_async_copy(a, b, sems.at[k]) for k, (a, b) in enumerate(pairs)]
    for copy in copies:
        copy.start()
    for copy in copies:
        copy.wait()


def finish(results):
    hbm = pl.BlockSpec(memory_space=pl.ANY)
    return pl.pallas_call(
        hand_over,
        out_shape=[jax.ShapeDtypeStruct(results[k].shape, F32) for k in (2, 3, 0, 1)],
        in_specs=[pl.BlockSpec(memory_space=pltpu.VMEM)] * 4,
        out_specs=[hbm] * 4,
        scratch_shapes=[pltpu.SemaphoreType.DMA((4,))],
        compiler_params=pltpu.CompilerParams(vmem_limit_bytes=LIMIT),
        name="hand_over",
    )(*results)


def body(x_block, hx_block, p_block, hp_block, tile_values, tile_rows, tile_cols, tile_count, coeffs):
    rows_n, cols_n = lax.axis_size("row"), lax.axis_size("col")
    states, length = x_block.shape
    slots = tile_values.shape[0]
    vmem = pl.BlockSpec(memory_space=pltpu.VMEM)
    word = jnp.int16
    hbm = pl.BlockSpec(memory_space=pl.ANY)
    outs = pl.pallas_call(
        functools.partial(kernel, rows_n, cols_n, length * rows_n * cols_n, slots),
        out_shape=(
            jax.ShapeDtypeStruct((states, length), F32),
            jax.ShapeDtypeStruct((states, length), F32),
            jax.ShapeDtypeStruct((24, 24), F32),
            jax.ShapeDtypeStruct((24, 24), F32),
        ),
        in_specs=[hbm] * 9,
        out_specs=(vmem,) * 4,
        scratch_shapes=[
            *[pltpu.VMEM((states, length), F32)] * 4,
            pltpu.VMEM(tile_values.shape, BF16),
            pltpu.SMEM((slots,), jnp.int32),
            pltpu.SMEM((slots,), jnp.int32),
            pltpu.SMEM((1,), jnp.int32),
            pltpu.VMEM((states, 24), F32),
            pltpu.VMEM((1, 128), F32),
            pltpu.VMEM((cols_n, 1, 128), F32),
            pltpu.VMEM((rows_n, 1, 128), F32),
            pltpu.VMEM((1, 128), F32),
            pltpu.VMEM((rows_n, 1, 128), F32),
            pltpu.VMEM((16, 128), word),
            pltpu.VMEM((cols_n, 16, 128), word),
            pltpu.VMEM((rows_n, 16, 128), word),
            pltpu.VMEM((32, 128), word),
            pltpu.VMEM((cols_n, 32, 128), word),
            pltpu.VMEM((rows_n, 32, 128), word),
            pltpu.VMEM((4, 8, 128), F32),
            pltpu.VMEM((rows_n // near_of(rows_n), 8, 128), F32),
            pltpu.VMEM((near_of(rows_n), 8, 128), F32),
            pltpu.VMEM((near_of(cols_n), 8, 128), F32),
            pltpu.VMEM((cols_n // near_of(cols_n), 8, 128), F32),
            pltpu.VMEM((2, 128), F32),
            pltpu.VMEM((rows_n, 2, 128), F32),
            pltpu.VMEM((2, 128), F32),
            pltpu.VMEM((cols_n, 2, 128), F32),
            pltpu.VMEM((cols_n, 16, 128), BF16),
            pltpu.VMEM((rows_n, 16, 128), BF16),
            pltpu.VMEM((cols_n, 16, 128), BF16),
            pltpu.VMEM((rows_n, 16, 128), BF16),
            pltpu.SemaphoreType.DMA((9,)),
            pltpu.SemaphoreType.DMA((19,)),
            pltpu.SemaphoreType.DMA((19,)),
        ],
        compiler_params=pltpu.CompilerParams(
            collective_id=0, has_side_effects=True, vmem_limit_bytes=LIMIT
        ),
        name="step",
    )(x_block, hx_block, p_block, hp_block, tile_values, tile_rows, tile_cols, tile_count, coeffs.T)
    return finish(outs)


def solution(mesh):
    both = ("row", "col")
    return jax.shard_map(
        body,
        mesh=mesh,
        in_specs=(
            P(None, both), P(None, both), P(None, both), P(None, both),
            P(both, None, None), P(both), P(both), P(both), P(),
        ),
        out_specs=(P(), P(), P(None, both), P(None, both)),
        check_vma=False,
    )
```

```python
import functools

import jax
import jax.numpy as jnp
from jax import lax
from jax.experimental import pallas as pl
from jax.experimental.pallas import tpu as pltpu
from jax.sharding import PartitionSpec as P

MESH = pl.DeviceIdType.MESH
F32 = jnp.float32
BF16 = jnp.bfloat16
EXACT = lax.Precision.HIGHEST
LEVELS = 32767.0
LIMIT = 60 << 20
NT = (((1,), (1,)), ((), ()))
NN = (((1,), (0,)), ((), ()))


def iota(shape, axis):
    return lax.broadcasted_iota(jnp.int32, shape, axis)


def dot(a, b, dims, precision=None):
    return lax.dot_general(a, b, dims, precision=precision, preferred_element_type=F32)


def to_row(columns):
    lane, sub = iota((8, 128), 1), iota((8, 128), 0)
    total = jnp.zeros((8, 128), F32)
    for place, column in enumerate(columns):
        total = total + jnp.where(lane == sub + 8 * place, column, 0.0)
    return jnp.sum(total, axis=0, keepdims=True)


def from_row(row, place):
    lane, sub = iota((8, 128), 1), iota((8, 128), 0)
    return jnp.sum(jnp.where(lane == sub + 8 * place, row, 0.0), axis=1, keepdims=True)


def halves(v):
    return v[:, :128], v[:, 128:]


def coded(v):
    top = jnp.max(jnp.abs(v), axis=1, keepdims=True)
    usable = top > 1e-30
    inverse = jnp.where(usable, LEVELS / jnp.where(usable, top, 1.0), 0.0)
    return jnp.round(v * inverse), top * (1.0 / LEVELS)


def split(v):
    high = v.astype(BF16)
    return high, (v - high.astype(F32)).astype(BF16)


def wait(ref, sem):
    pltpu.make_async_copy(ref, ref, sem).wait()


def near_of(n):
    return 4 if n >= 16 else 2


def kernel(
    rows_n, cols_n, cells, slots,
    x_hbm, hx_hbm, p_hbm, hp_hbm, tiles_hbm, rows_hbm, cols_hbm, count_hbm, coef_hbm,
    xn_ref, hxn_ref, gh_ref, gs_ref,
    x_ref, hx_ref, p_ref, hp_ref, tiles, rows_ref, cols_ref, count_ref, coef_ref,
    stat, rstat, cstat, csum, csums, near_send, rnear, cnear, pair_send, rpair, cpair,
    early, early_x, early_q, early_h, early_z, late, lrow, lsum, lcol, rsend, csend, rrecv, crecv,
    load, send, recv,
):
    r, c = lax.axis_index("row"), lax.axis_index("col")
    near_n, high_n = near_of(rows_n), near_of(cols_n)
    x_n, z_n = rows_n // near_n, cols_n // high_n
    my_x, my_q = r // near_n, lax.rem(r, near_n)
    my_h, my_z = c // z_n, lax.rem(c, z_n)
    my_slot = my_z * high_n + my_h
    my_near = my_q * x_n + my_x

    def along_col(i):
        return lax.rem(c + 1 + i, cols_n)

    def along_row(i):
        return lax.rem(r + 1 + i, rows_n)

    def each(n, f):
        def step(i, carry):
            f(i)
            return carry
        lax.fori_loop(0, n - 1, step, 0)

    def push(src, dst, k, axis, j):
        pltpu.make_async_remote_copy(
            src_ref=src, dst_ref=dst, send_sem=send.at[k], recv_sem=recv.at[k],
            device_id={axis: j}, device_id_type=MESH,
        ).start()

    def offsets(n, f):
        for i in range(1, n):
            f(i)

    def at_x(i):
        return lax.rem(my_x + i, x_n) * near_n + my_q

    def at_q(i):
        return my_x * near_n + lax.rem(my_q + i, near_n)

    def at_z(i):
        return my_h * z_n + lax.rem(my_z + i, z_n)

    def at_h(i):
        return lax.rem(my_h + i, high_n) * z_n + my_z

    table = (
        (0, rstat, z_n - 1), (20, rstat, cols_n - z_n), (1, cstat, x_n - 1), (19, cstat, rows_n - x_n), (4, csums, rows_n - 1),
        (5, cpair, near_n - 1), (13, cpair, rows_n - near_n), (6, rpair, high_n - 1), (14, rpair, cols_n - high_n),
        (3, cnear, x_n - 1), (18, cnear, rows_n - x_n), (2, rnear, z_n - 1), (17, rnear, cols_n - z_n),
        (16, early_z, z_n - 1), (15, early_h, high_n - 1), (11, early_x, x_n - 1), (12, early_q, near_n - 1),
        (7, lrow, rows_n - 1), (8, lcol, cols_n - 1), (9, rrecv, cols_n - 1), (10, crecv, rows_n - 1),
    )

    def arrive(k):
        ref, n = next((ref, n) for j, ref, n in table if j == k)
        wait(ref.at[pl.ds(0, n)], recv.at[k])

    loads = [
        pltpu.make_async_copy(a, b, load.at[k])
        for k, (a, b) in enumerate((
            (x_hbm, x_ref), (hx_hbm, hx_ref), (p_hbm, p_ref), (hp_hbm, hp_ref), (tiles_hbm, tiles),
            (rows_hbm, rows_ref), (cols_hbm, cols_ref), (count_hbm, count_ref), (coef_hbm, coef_ref)))
    ]
    for copy in loads:
        copy.start()
    groups = ((z_n, "col", at_z), (high_n, "col", at_h), (x_n, "row", at_x), (near_n, "row", at_q))
    barrier = pltpu.get_barrier_semaphore()
    for n, axis, at in groups:
        offsets(n, lambda i: pl.semaphore_signal(
            barrier, inc=1, device_id={axis: at(i)}, device_id_type=MESH))
    for k in (0, 1, 2, 3, 5, 6, 7, 8):
        loads[k].wait()

    x, hx, p, hp = x_ref[...], hx_ref[...], p_ref[...], hp_ref[...]
    cross = jnp.sum(x * hx, axis=1, keepdims=True)
    square = jnp.sum(x * x, axis=1, keepdims=True)
    some = square > 0.0
    guess = jnp.where(some, cross / jnp.where(some, square, 1.0), 0.0)
    near = hx - guess * x
    near_code, near_step = coded(near)
    x_code, x_step = coded(x)
    p_code, p_step = coded(p)
    row = to_row([cross, square, guess, near_step, x_step, p_step])
    stat[...] = row
    rstat[c] = row
    cstat[my_near] = row
    near_code = jnp.concatenate(halves(near_code), axis=0).astype(jnp.int32).astype(jnp.int16)
    near_send[...] = near_code
    rnear[c] = near_code
    cnear[my_near] = near_code
    pair = jnp.concatenate(halves(x_code) + halves(p_code), axis=0).astype(jnp.int32).astype(jnp.int16)
    pair_send[...] = pair
    rpair[my_slot] = pair
    cpair[r] = pair

    pl.semaphore_wait(barrier, sum(n - 1 for n, _, _ in groups))

    offsets(z_n, lambda i: push(stat, rstat.at[c], 0, "col", at_z(i)))
    offsets(high_n, lambda i: push(pair_send, rpair.at[my_slot], 6, "col", at_h(i)))
    offsets(near_n, lambda i: push(pair_send, cpair.at[r], 5, "row", at_q(i)))
    offsets(z_n, lambda i: push(near_send, rnear.at[c], 2, "col", at_z(i)))
    offsets(x_n, lambda i: push(near_send, cnear.at[my_near], 3, "row", at_x(i)))
    offsets(x_n, lambda i: push(stat, cstat.at[my_near], 1, "row", at_x(i)))

    lane, sub = iota((8, 128), 1), iota((8, 128), 0)
    own_state = lax.rem(lane, 8) == sub
    slot_of = lax.rem(lane, 8 * slots) // 8

    def onehot(ids, n):
        place = jnp.zeros((8, 128), jnp.int32)
        for s in range(slots):
            place = jnp.where(slot_of == s, ids[s], place)
        blocks = [jnp.where((place == d) & own_state, 1.0, 0.0) for d in range(n)]
        return jnp.concatenate(blocks, axis=0).astype(BF16)

    row_hot, col_hot = onehot(rows_ref, cols_n), onehot(cols_ref, rows_n)

    def onward(n, ref, first, size, k, axis, at):
        group = ref.at[pl.ds(first, size)]
        offsets(n, lambda i: push(group, group, k, axis, at(i)))

    arrive(5)
    onward(x_n, cpair, my_x * near_n, near_n, 13, "row", at_x)
    arrive(0)
    onward(high_n, rstat, my_h * z_n, z_n, 20, "col", at_h)
    arrive(6)
    onward(z_n, rpair, my_z * high_n, high_n, 14, "col", at_z)
    arrive(2)
    onward(high_n, rnear, my_h * z_n, z_n, 17, "col", at_h)
    arrive(3)
    onward(near_n, cnear, my_q * x_n, x_n, 18, "row", at_q)
    arrive(1)
    onward(near_n, cstat, my_q * x_n, x_n, 19, "row", at_q)

    arrive(20)
    col_total = jnp.sum(rstat[...], axis=0)
    csum[...] = col_total
    csums[r] = col_total
    each(rows_n, lambda i: push(csum, csums.at[r], 4, "row", along_row(i)))
    row_cross, row_square = from_row(col_total, 0), from_row(col_total, 1)
    some = row_square > 0.0
    row_theta = jnp.where(some, row_cross / jnp.where(some, row_square, 1.0), 0.0)
    basis = jnp.concatenate([x, hx - row_theta * x, p], axis=0)
    others = jnp.concatenate([basis, hx, hp, jnp.zeros((88, x.shape[1]), F32)], axis=0)
    products = dot(basis, others, NT, EXACT)
    tile = (products[0:8] + pltpu.roll(products[8:16], 40, 1)) + pltpu.roll(products[16:24], 80, 1)
    early[0] = tile
    early_z[my_z] = tile
    offsets(z_n, lambda i: push(early.at[0], early_z.at[my_z], 16, "col", at_z(i)))

    arrive(19)

    def near_slot(at):
        return lax.rem(at, near_n) * x_n + at // near_n

    def numbers(row):
        return [from_row(row, place) for place in (2, 3, 4, 5)]

    col_numbers = [numbers(cstat[near_slot(cols_ref[s])]) for s in range(slots)]
    row_numbers = [numbers(rstat[rows_ref[s]]) for s in range(slots)]

    def early_step(k, n, gathered):
        arrive(k)
        return jnp.sum(gathered[...], axis=0)

    tile = early_step(16, z_n, early_z)
    early[1] = tile
    early_h[my_h] = tile
    offsets(high_n, lambda i: push(early.at[1], early_h.at[my_h], 15, "col", at_h(i)))

    arrive(4)
    total = jnp.sum(csums[...], axis=0)
    theta = from_row(total, 0) / from_row(total, 1)
    residual = hx - theta * x
    basis = jnp.concatenate([x, residual, p], axis=0)

    for k in (18, 17, 13, 14):
        arrive(k)
    loads[4].wait()

    def fetch(numbers, near_words, pair_words):
        guess, near_part, x_part, p_part = numbers
        near_code = near_words.astype(jnp.int32).astype(F32)
        pair_code = pair_words.astype(jnp.int32).astype(F32)
        x_wide = jnp.concatenate([pair_code[0:8], pair_code[8:16]], axis=1)
        p_wide = jnp.concatenate([pair_code[16:24], pair_code[24:32]], axis=1)
        near_wide = jnp.concatenate([near_code[0:8], near_code[8:16]], axis=1)
        res = near_part * near_wide + ((guess - theta) * x_part) * x_wide
        return res, jnp.concatenate([x_part * x_wide, res, p_part * p_wide], axis=0)

    forward, mirror, left, right = [], [], [], []
    for s in range(slots):
        live = jnp.where(s < count_ref[0], 1.0, 0.0).astype(F32)
        at_col, at_row = cols_ref[s], rows_ref[s]
        by_col, col_basis = fetch(
            col_numbers[s], cnear[near_slot(at_col)], cpair[at_col])
        by_row, row_basis = fetch(
            row_numbers[s], rnear[at_row], rpair[lax.rem(at_row, z_n) * high_n + at_row // z_n])
        matrix = tiles[s]
        forward.append(split(dot(by_col.astype(BF16), matrix, NT) * live))
        mirror.append(split(dot(by_row.astype(BF16), matrix, NN) * live))
        left += [jnp.concatenate(forward[-1], axis=0), jnp.concatenate(mirror[-1], axis=0)]
        right += [jnp.concatenate(split(row_basis), axis=0), jnp.concatenate(split(col_basis), axis=0)]
    partial = dot(jnp.concatenate(left, axis=1), jnp.concatenate(right, axis=1), NT)

    g = partial[0:8] + partial[8:16]
    from_lane = iota((48, 256), 0)
    to_lane = lax.rem(iota((48, 256), 1), 32)
    spread = jnp.where((from_lane == to_lane) & (to_lane < 24) | (from_lane == to_lane + 24) & (to_lane < 24), 1.0, 0.0)
    g = dot(g, spread, NN, EXACT)
    g = jnp.sum(jnp.where(iota((8, 256), 1) // 32 == iota((8, 256), 0), g, 0.0), axis=0, keepdims=True)
    flat = jnp.concatenate([g[:, :128], g[:, 128:]], axis=0)
    late[...] = flat
    lrow[r] = flat
    each(rows_n, lambda i: push(late, lrow.at[r], 7, "row", along_row(i)))

    def spread_out(hot, parts, n, buffer):
        stack = jnp.concatenate([h for h, _ in parts] + [l for _, l in parts], axis=0)
        out = dot(hot, stack, NN)
        left, right = halves(out)
        out = jnp.concatenate([left.reshape(n, 8, 128), right.reshape(n, 8, 128)], axis=1)
        buffer[...] = out.astype(BF16)

    spread_out(row_hot, forward, cols_n, rsend)
    spread_out(col_hot, mirror, rows_n, csend)

    def push_parts(i):
        j, k = along_col(i), along_row(i)
        push(rsend.at[j], rrecv.at[c], 9, "col", j)
        push(csend.at[k], crecv.at[r], 10, "row", k)

    each(cols_n, push_parts)
    rrecv[c] = rsend[c]
    crecv[r] = csend[r]

    tile = early_step(15, high_n, early_h)
    shift = row_theta - theta
    in_rows = (lane >= 40) & (lane < 80)
    tile = tile + jnp.where(in_rows, shift * pltpu.roll(tile, 40, 1), 0.0)
    columns = jnp.where(lax.rem(lane, 40) == sub + 8, shift, 0.0)
    tile = tile + jnp.sum(columns, axis=0, keepdims=True) * pltpu.roll(tile, 8, 1)
    early[2] = tile
    early_x[my_x] = tile
    offsets(x_n, lambda i: push(early.at[2], early_x.at[my_x], 11, "row", at_x(i)))

    arrive(7)
    flat = jnp.sum(lrow[...], axis=0)
    lsum[...] = flat
    lcol[c] = flat
    each(cols_n, lambda i: push(lsum, lcol.at[c], 8, "col", along_col(i)))

    tile = early_step(11, x_n, early_x)
    early[3] = tile
    early_q[my_q] = tile
    offsets(near_n, lambda i: push(early.at[3], early_q.at[my_q], 12, "row", at_q(i)))

    coef = coef_ref[...]
    xn_ref[...] = dot(coef, basis, NN, EXACT)

    arrive(9)
    arrive(10)
    image = jnp.sum(rrecv[...].astype(F32), axis=0) + jnp.sum(crecv[...].astype(F32), axis=0)
    image = jnp.concatenate([image[0:8], image[8:16]], axis=1)
    hxn_ref[...] = dot(coef, jnp.concatenate([hx, image, hp], axis=0), NN, EXACT)

    scale = 1.0 / cells
    tile = early_step(12, near_n, early_q)
    products = jnp.concatenate([tile, pltpu.roll(tile, 88, 1), pltpu.roll(tile, 48, 1)], axis=0) * scale
    gs_ref[...] = products[:, :24]

    arrive(8)
    flat = jnp.sum(lcol[...], axis=0)
    flat = jnp.concatenate([flat[0:1], flat[1:2]], axis=1)
    mine = lax.rem(iota((24, 256), 1), 32) == iota((24, 256), 0)
    gather = jnp.where(iota((256, 128), 1) == 8 + iota((256, 128), 0) // 32, scale, 0.0)
    middle = dot(jnp.where(mine, flat, 0.0), gather, NN, EXACT)
    at = iota((24, 128), 1)
    full = jnp.where(at < 8, pltpu.roll(products, 104, 1), jnp.where(at < 16, middle, pltpu.roll(products, 112, 1)))
    gh_ref[...] = full[:, :24]

    for k, ref, n in table:
        wait(ref.at[pl.ds(0, n)], send.at[k])


def hand_over(xn_ref, hxn_ref, gh_ref, gs_ref, gh_out, gs_out, xn_out, hxn_out, sems):
    pairs = ((gh_ref, gh_out), (gs_ref, gs_out), (xn_ref, xn_out), (hxn_ref, hxn_out))
    copies = [pltpu.make_async_copy(a, b, sems.at[k]) for k, (a, b) in enumerate(pairs)]
    for copy in copies:
        copy.start()
    for copy in copies:
        copy.wait()


def finish(results):
    hbm = pl.BlockSpec(memory_space=pl.ANY)
    return pl.pallas_call(
        hand_over,
        out_shape=[jax.ShapeDtypeStruct(results[k].shape, F32) for k in (2, 3, 0, 1)],
        in_specs=[pl.BlockSpec(memory_space=pltpu.VMEM)] * 4,
        out_specs=[hbm] * 4,
        scratch_shapes=[pltpu.SemaphoreType.DMA((4,))],
        compiler_params=pltpu.CompilerParams(vmem_limit_bytes=1 << 20),
        name="hand_over",
    )(*results)


def body(x_block, hx_block, p_block, hp_block, tile_values, tile_rows, tile_cols, tile_count, coeffs):
    rows_n, cols_n = lax.axis_size("row"), lax.axis_size("col")
    states, length = x_block.shape
    slots = tile_values.shape[0]
    vmem = pl.BlockSpec(memory_space=pltpu.VMEM)
    word = jnp.int16
    hbm = pl.BlockSpec(memory_space=pl.ANY)
    outs = pl.pallas_call(
        functools.partial(kernel, rows_n, cols_n, length * rows_n * cols_n, slots),
        out_shape=(
            pltpu.VMEM((states, length), F32),
            pltpu.VMEM((states, length), F32),
            pltpu.VMEM((24, 24), F32),
            pltpu.VMEM((24, 24), F32),
        ),
        in_specs=[hbm] * 9,
        out_specs=(vmem,) * 4,
        scratch_shapes=[
            *[pltpu.VMEM((states, length), F32)] * 4,
            pltpu.VMEM(tile_values.shape, BF16),
            pltpu.SMEM((slots,), jnp.int32),
            pltpu.SMEM((slots,), jnp.int32),
            pltpu.SMEM((1,), jnp.int32),
            pltpu.VMEM((states, 24), F32),
            pltpu.VMEM((1, 128), F32),
            pltpu.VMEM((cols_n, 1, 128), F32),
            pltpu.VMEM((rows_n, 1, 128), F32),
            pltpu.VMEM((1, 128), F32),
            pltpu.VMEM((rows_n, 1, 128), F32),
            pltpu.VMEM((16, 128), word),
            pltpu.VMEM((cols_n, 16, 128), word),
            pltpu.VMEM((rows_n, 16, 128), word),
            pltpu.VMEM((32, 128), word),
            pltpu.VMEM((cols_n, 32, 128), word),
            pltpu.VMEM((rows_n, 32, 128), word),
            pltpu.VMEM((4, 8, 128), F32),
            pltpu.VMEM((rows_n // near_of(rows_n), 8, 128), F32),
            pltpu.VMEM((near_of(rows_n), 8, 128), F32),
            pltpu.VMEM((near_of(cols_n), 8, 128), F32),
            pltpu.VMEM((cols_n // near_of(cols_n), 8, 128), F32),
            pltpu.VMEM((2, 128), F32),
            pltpu.VMEM((rows_n, 2, 128), F32),
            pltpu.VMEM((2, 128), F32),
            pltpu.VMEM((cols_n, 2, 128), F32),
            pltpu.VMEM((cols_n, 16, 128), BF16),
            pltpu.VMEM((rows_n, 16, 128), BF16),
            pltpu.VMEM((cols_n, 16, 128), BF16),
            pltpu.VMEM((rows_n, 16, 128), BF16),
            pltpu.SemaphoreType.DMA((9,)),
            pltpu.SemaphoreType.DMA((21,)),
            pltpu.SemaphoreType.DMA((21,)),
        ],
        compiler_params=pltpu.CompilerParams(
            collective_id=0, has_side_effects=True, vmem_limit_bytes=LIMIT
        ),
        name="step",
    )(x_block, hx_block, p_block, hp_block, tile_values, tile_rows, tile_cols, tile_count, coeffs.T)
    return finish(outs)


def solution(mesh):
    both = ("row", "col")
    return jax.shard_map(
        body,
        mesh=mesh,
        in_specs=(
            P(None, both), P(None, both), P(None, both), P(None, both),
            P(both, None, None), P(both), P(both), P(both), P(),
        ),
        out_specs=(P(), P(), P(None, both), P(None, both)),
        check_vma=False,
    )
```

```python
import functools

import jax
import jax.numpy as jnp
from jax import lax
from jax.experimental import pallas as pl
from jax.experimental.pallas import tpu as pltpu
from jax.sharding import PartitionSpec as P

MESH = pl.DeviceIdType.MESH
F32 = jnp.float32
BF16 = jnp.bfloat16
EXACT = lax.Precision.HIGHEST
LEVELS = 32767.0
LIMIT = 60 << 20
NT = (((1,), (1,)), ((), ()))
NN = (((1,), (0,)), ((), ()))


def iota(shape, axis):
    return lax.broadcasted_iota(jnp.int32, shape, axis)


def dot(a, b, dims, precision=None):
    return lax.dot_general(a, b, dims, precision=precision, preferred_element_type=F32)


def to_row(columns):
    lane, sub = iota((8, 128), 1), iota((8, 128), 0)
    total = jnp.zeros((8, 128), F32)
    for place, column in enumerate(columns):
        total = total + jnp.where(lane == sub + 8 * place, column, 0.0)
    return jnp.sum(total, axis=0, keepdims=True)


def from_row(row, place):
    lane, sub = iota((8, 128), 1), iota((8, 128), 0)
    return jnp.sum(jnp.where(lane == sub + 8 * place, row, 0.0), axis=1, keepdims=True)


def halves(v):
    return v[:, :128], v[:, 128:]


def coded(v):
    top = jnp.max(jnp.abs(v), axis=1, keepdims=True)
    usable = top > 1e-30
    inverse = jnp.where(usable, LEVELS / jnp.where(usable, top, 1.0), 0.0)
    return jnp.round(v * inverse), top * (1.0 / LEVELS)


def split(v):
    high = v.astype(BF16)
    return high, (v - high.astype(F32)).astype(BF16)


def wait(ref, sem):
    pltpu.make_async_copy(ref, ref, sem).wait()


def near_of(n):
    return 4 if n >= 16 else 2


def kernel(
    rows_n, cols_n, cells, slots,
    x_hbm, hx_hbm, p_hbm, hp_hbm, tiles_hbm, rows_hbm, cols_hbm, count_hbm, coef_hbm,
    xn_ref, hxn_ref, gh_ref, gs_ref,
    x_ref, hx_ref, p_ref, hp_ref, tiles, rows_ref, cols_ref, count_ref, coef_ref,
    stat, rstat, cstat, csum, csums, near_send, rnear, cnear, pair_send, rpair, cpair,
    early, early_x, early_q, early_h, early_z, late, lrow, lsum, lcol, rsend, csend, rrecv, crecv,
    load, send, recv,
):
    r, c = lax.axis_index("row"), lax.axis_index("col")
    near_n, high_n = near_of(rows_n), near_of(cols_n)
    x_n, z_n = rows_n // near_n, cols_n // high_n
    my_x, my_q = r // near_n, lax.rem(r, near_n)
    my_h, my_z = c // z_n, lax.rem(c, z_n)
    my_slot = my_z * high_n + my_h
    my_near = my_q * x_n + my_x

    def along_col(i):
        return lax.rem(c + 1 + i, cols_n)

    def along_row(i):
        return lax.rem(r + 1 + i, rows_n)

    def each(n, f):
        def step(i, carry):
            f(i)
            return carry
        lax.fori_loop(0, n - 1, step, 0)

    def push(src, dst, k, axis, j):
        pltpu.make_async_remote_copy(
            src_ref=src, dst_ref=dst, send_sem=send.at[k], recv_sem=recv.at[k],
            device_id={axis: j}, device_id_type=MESH,
        ).start()

    def offsets(n, f):
        for i in sorted(range(1, n), key=lambda i: -min(i, n - i)):
            f(i)

    def at_x(i):
        return lax.rem(my_x + i, x_n) * near_n + my_q

    def at_q(i):
        return my_x * near_n + lax.rem(my_q + i, near_n)

    def at_z(i):
        return my_h * z_n + lax.rem(my_z + i, z_n)

    def at_h(i):
        return lax.rem(my_h + i, high_n) * z_n + my_z

    table = (
        (0, rstat, z_n - 1), (20, rstat, cols_n - z_n), (1, cstat, x_n - 1), (19, cstat, rows_n - x_n), (4, csums, rows_n - 1),
        (5, cpair, near_n - 1), (13, cpair, rows_n - near_n), (6, rpair, high_n - 1), (14, rpair, cols_n - high_n),
        (3, cnear, x_n - 1), (18, cnear, rows_n - x_n), (2, rnear, z_n - 1), (17, rnear, cols_n - z_n),
        (16, early_z, z_n - 1), (15, early_h, high_n - 1), (11, early_x, x_n - 1), (12, early_q, near_n - 1),
        (7, lrow, rows_n - 1), (8, lcol, cols_n - 1), (9, rrecv, cols_n - 1), (10, crecv, rows_n - 1),
    )

    def arrive(k):
        ref, n = next((ref, n) for j, ref, n in table if j == k)
        wait(ref.at[pl.ds(0, n)], recv.at[k])

    groups = ((z_n, "col", at_z), (high_n, "col", at_h), (x_n, "row", at_x), (near_n, "row", at_q))
    barrier = pltpu.get_barrier_semaphore()
    for n, axis, at in groups:
        offsets(n, lambda i: pl.semaphore_signal(
            barrier, inc=1, device_id={axis: at(i)}, device_id_type=MESH))
    loads = [
        pltpu.make_async_copy(a, b, load.at[k])
        for k, (a, b) in enumerate((
            (x_hbm, x_ref), (hx_hbm, hx_ref), (p_hbm, p_ref), (hp_hbm, hp_ref), (tiles_hbm, tiles),
            (rows_hbm, rows_ref), (cols_hbm, cols_ref), (count_hbm, count_ref), (coef_hbm, coef_ref)))
    ]
    for copy in loads:
        copy.start()
    for k in (0, 1, 2, 3, 5, 6, 7, 8):
        loads[k].wait()

    x, hx, p, hp = x_ref[...], hx_ref[...], p_ref[...], hp_ref[...]
    cross = jnp.sum(x * hx, axis=1, keepdims=True)
    square = jnp.sum(x * x, axis=1, keepdims=True)
    some = square > 0.0
    guess = jnp.where(some, cross / jnp.where(some, square, 1.0), 0.0)
    near = hx - guess * x
    near_code, near_step = coded(near)
    x_code, x_step = coded(x)
    p_code, p_step = coded(p)
    row = to_row([cross, square, guess, near_step, x_step, p_step])
    stat[...] = row
    rstat[c] = row
    cstat[my_near] = row
    near_code = jnp.concatenate(halves(near_code), axis=0).astype(jnp.int32).astype(jnp.int16)
    near_send[...] = near_code
    rnear[c] = near_code
    cnear[my_near] = near_code
    pair = jnp.concatenate(halves(x_code) + halves(p_code), axis=0).astype(jnp.int32).astype(jnp.int16)
    pair_send[...] = pair
    rpair[my_slot] = pair
    cpair[r] = pair

    pl.semaphore_wait(barrier, sum(n - 1 for n, _, _ in groups))

    offsets(z_n, lambda i: push(stat, rstat.at[c], 0, "col", at_z(i)))
    offsets(high_n, lambda i: push(pair_send, rpair.at[my_slot], 6, "col", at_h(i)))
    offsets(near_n, lambda i: push(pair_send, cpair.at[r], 5, "row", at_q(i)))
    offsets(z_n, lambda i: push(near_send, rnear.at[c], 2, "col", at_z(i)))
    offsets(x_n, lambda i: push(near_send, cnear.at[my_near], 3, "row", at_x(i)))
    offsets(x_n, lambda i: push(stat, cstat.at[my_near], 1, "row", at_x(i)))

    lane, sub = iota((8, 128), 1), iota((8, 128), 0)
    own_state = lax.rem(lane, 8) == sub
    slot_of = lax.rem(lane, 8 * slots) // 8

    def onehot(ids, n):
        place = jnp.zeros((8, 128), jnp.int32)
        for s in range(slots):
            place = jnp.where(slot_of == s, ids[s], place)
        blocks = [jnp.where((place == d) & own_state, 1.0, 0.0) for d in range(n)]
        return jnp.concatenate(blocks, axis=0).astype(BF16)

    row_hot, col_hot = onehot(rows_ref, cols_n), onehot(cols_ref, rows_n)

    def onward(n, ref, first, size, k, axis, at):
        group = ref.at[pl.ds(first, size)]
        offsets(n, lambda i: push(group, group, k, axis, at(i)))

    arrive(5)
    onward(x_n, cpair, my_x * near_n, near_n, 13, "row", at_x)
    arrive(0)
    onward(high_n, rstat, my_h * z_n, z_n, 20, "col", at_h)
    arrive(6)
    onward(z_n, rpair, my_z * high_n, high_n, 14, "col", at_z)
    arrive(2)
    onward(high_n, rnear, my_h * z_n, z_n, 17, "col", at_h)
    arrive(3)
    onward(near_n, cnear, my_q * x_n, x_n, 18, "row", at_q)
    arrive(1)
    onward(near_n, cstat, my_q * x_n, x_n, 19, "row", at_q)

    arrive(20)
    col_total = jnp.sum(rstat[...], axis=0)
    csum[...] = col_total
    csums[r] = col_total
    each(rows_n, lambda i: push(csum, csums.at[r], 4, "row", along_row(i)))
    row_cross, row_square = from_row(col_total, 0), from_row(col_total, 1)
    some = row_square > 0.0
    row_theta = jnp.where(some, row_cross / jnp.where(some, row_square, 1.0), 0.0)
    basis = jnp.concatenate([x, hx - row_theta * x, p], axis=0)
    others = jnp.concatenate([basis, hx, hp, jnp.zeros((88, x.shape[1]), F32)], axis=0)
    products = dot(basis, others, NT, EXACT)
    tile = (products[0:8] + pltpu.roll(products[8:16], 40, 1)) + pltpu.roll(products[16:24], 80, 1)
    early[0] = tile
    early_z[my_z] = tile
    offsets(z_n, lambda i: push(early.at[0], early_z.at[my_z], 16, "col", at_z(i)))

    arrive(19)

    def near_slot(at):
        return lax.rem(at, near_n) * x_n + at // near_n

    def numbers(row):
        return [from_row(row, place) for place in (2, 3, 4, 5)]

    col_numbers = [numbers(cstat[near_slot(cols_ref[s])]) for s in range(slots)]
    row_numbers = [numbers(rstat[rows_ref[s]]) for s in range(slots)]

    def early_step(k, n, gathered):
        arrive(k)
        return jnp.sum(gathered[...], axis=0)

    tile = early_step(16, z_n, early_z)
    early[1] = tile
    early_h[my_h] = tile
    offsets(high_n, lambda i: push(early.at[1], early_h.at[my_h], 15, "col", at_h(i)))

    arrive(4)
    total = jnp.sum(csums[...], axis=0)
    theta = from_row(total, 0) / from_row(total, 1)
    residual = hx - theta * x
    basis = jnp.concatenate([x, residual, p], axis=0)

    for k in (18, 17, 13, 14):
        arrive(k)
    loads[4].wait()

    def fetch(numbers, near_words, pair_words):
        guess, near_part, x_part, p_part = numbers
        near_code = near_words.astype(jnp.int32).astype(F32)
        pair_code = pair_words.astype(jnp.int32).astype(F32)
        x_wide = jnp.concatenate([pair_code[0:8], pair_code[8:16]], axis=1)
        p_wide = jnp.concatenate([pair_code[16:24], pair_code[24:32]], axis=1)
        near_wide = jnp.concatenate([near_code[0:8], near_code[8:16]], axis=1)
        res = near_part * near_wide + ((guess - theta) * x_part) * x_wide
        return res, jnp.concatenate([x_part * x_wide, res, p_part * p_wide], axis=0)

    forward, mirror, left, right = [], [], [], []
    for s in range(slots):
        live = jnp.where(s < count_ref[0], 1.0, 0.0).astype(F32)
        at_col, at_row = cols_ref[s], rows_ref[s]
        by_col, col_basis = fetch(
            col_numbers[s], cnear[near_slot(at_col)], cpair[at_col])
        by_row, row_basis = fetch(
            row_numbers[s], rnear[at_row], rpair[lax.rem(at_row, z_n) * high_n + at_row // z_n])
        matrix = tiles[s]
        forward.append(split(dot(by_col.astype(BF16), matrix, NT) * live))
        mirror.append(split(dot(by_row.astype(BF16), matrix, NN) * live))
        left += [jnp.concatenate(forward[-1], axis=0), jnp.concatenate(mirror[-1], axis=0)]
        right += [jnp.concatenate(split(row_basis), axis=0), jnp.concatenate(split(col_basis), axis=0)]
    partial = dot(jnp.concatenate(left, axis=1), jnp.concatenate(right, axis=1), NT)

    g = partial[0:8] + partial[8:16]
    from_lane = iota((48, 256), 0)
    to_lane = lax.rem(iota((48, 256), 1), 32)
    spread = jnp.where((from_lane == to_lane) & (to_lane < 24) | (from_lane == to_lane + 24) & (to_lane < 24), 1.0, 0.0)
    g = dot(g, spread, NN, EXACT)
    g = jnp.sum(jnp.where(iota((8, 256), 1) // 32 == iota((8, 256), 0), g, 0.0), axis=0, keepdims=True)
    flat = jnp.concatenate([g[:, :128], g[:, 128:]], axis=0)
    late[...] = flat
    lrow[r] = flat
    each(rows_n, lambda i: push(late, lrow.at[r], 7, "row", along_row(i)))

    def spread_out(hot, parts, n, buffer):
        stack = jnp.concatenate([h for h, _ in parts] + [l for _, l in parts], axis=0)
        out = dot(hot, stack, NN)
        left, right = halves(out)
        out = jnp.concatenate([left.reshape(n, 8, 128), right.reshape(n, 8, 128)], axis=1)
        buffer[...] = out.astype(BF16)

    spread_out(row_hot, forward, cols_n, rsend)
    spread_out(col_hot, mirror, rows_n, csend)

    def push_parts(i):
        j, k = along_col(i), along_row(i)
        push(rsend.at[j], rrecv.at[c], 9, "col", j)
        push(csend.at[k], crecv.at[r], 10, "row", k)

    each(cols_n, push_parts)
    rrecv[c] = rsend[c]
    crecv[r] = csend[r]

    tile = early_step(15, high_n, early_h)
    shift = row_theta - theta
    in_rows = (lane >= 40) & (lane < 80)
    tile = tile + jnp.where(in_rows, shift * pltpu.roll(tile, 40, 1), 0.0)
    columns = jnp.where(lax.rem(lane, 40) == sub + 8, shift, 0.0)
    tile = tile + jnp.sum(columns, axis=0, keepdims=True) * pltpu.roll(tile, 8, 1)
    early[2] = tile
    early_x[my_x] = tile
    offsets(x_n, lambda i: push(early.at[2], early_x.at[my_x], 11, "row", at_x(i)))

    arrive(7)
    flat = jnp.sum(lrow[...], axis=0)
    lsum[...] = flat
    lcol[c] = flat
    each(cols_n, lambda i: push(lsum, lcol.at[c], 8, "col", along_col(i)))

    tile = early_step(11, x_n, early_x)
    early[3] = tile
    early_q[my_q] = tile
    offsets(near_n, lambda i: push(early.at[3], early_q.at[my_q], 12, "row", at_q(i)))

    coef = coef_ref[...]
    xn_ref[...] = dot(coef, basis, NN, EXACT)

    scale = 1.0 / cells
    tile = early_step(12, near_n, early_q)
    products = jnp.concatenate([tile, pltpu.roll(tile, 88, 1), pltpu.roll(tile, 48, 1)], axis=0) * scale
    gs_ref[...] = products[:, :24]
    at = iota((24, 128), 1)
    outer = jnp.where(at < 8, pltpu.roll(products, 104, 1), pltpu.roll(products, 112, 1))
    known = dot(coef, jnp.concatenate([hx, jnp.zeros_like(hx), hp], axis=0), NN, EXACT)

    for k in (9, 10, 8):
        arrive(k)
    image = jnp.sum(rrecv[...].astype(F32), axis=0) + jnp.sum(crecv[...].astype(F32), axis=0)
    image = jnp.concatenate([image[0:8], image[8:16]], axis=1)
    hxn_ref[...] = known + dot(coef[:, 8:16], image, NN, EXACT)
    flat = jnp.sum(lcol[...], axis=0)
    flat = jnp.concatenate([flat[0:1], flat[1:2]], axis=1)
    mine = lax.rem(iota((24, 256), 1), 32) == iota((24, 256), 0)
    gather = jnp.where(iota((256, 128), 1) == 8 + iota((256, 128), 0) // 32, scale, 0.0)
    middle = dot(jnp.where(mine, flat, 0.0), gather, NN, EXACT)
    gh_ref[...] = jnp.where((at >= 8) & (at < 16), middle, outer)[:, :24]

    for k, ref, n in table:
        wait(ref.at[pl.ds(0, n)], send.at[k])


def hand_over(xn_ref, hxn_ref, gh_ref, gs_ref, gh_out, gs_out, xn_out, hxn_out, sems):
    pairs = ((gh_ref, gh_out), (gs_ref, gs_out), (xn_ref, xn_out), (hxn_ref, hxn_out))
    copies = [pltpu.make_async_copy(a, b, sems.at[k]) for k, (a, b) in enumerate(pairs)]
    for copy in copies:
        copy.start()
    for copy in copies:
        copy.wait()


def finish(results):
    hbm = pl.BlockSpec(memory_space=pl.ANY)
    return pl.pallas_call(
        hand_over,
        out_shape=[jax.ShapeDtypeStruct(results[k].shape, F32) for k in (2, 3, 0, 1)],
        in_specs=[pl.BlockSpec(memory_space=pltpu.VMEM)] * 4,
        out_specs=[hbm] * 4,
        scratch_shapes=[pltpu.SemaphoreType.DMA((4,))],
        compiler_params=pltpu.CompilerParams(vmem_limit_bytes=1 << 20),
        name="hand_over",
    )(*results)


def body(x_block, hx_block, p_block, hp_block, tile_values, tile_rows, tile_cols, tile_count, coeffs):
    rows_n, cols_n = lax.axis_size("row"), lax.axis_size("col")
    states, length = x_block.shape
    slots = tile_values.shape[0]
    vmem = pl.BlockSpec(memory_space=pltpu.VMEM)
    word = jnp.int16
    hbm = pl.BlockSpec(memory_space=pl.ANY)
    outs = pl.pallas_call(
        functools.partial(kernel, rows_n, cols_n, length * rows_n * cols_n, slots),
        out_shape=(
            pltpu.VMEM((states, length), F32),
            pltpu.VMEM((states, length), F32),
            pltpu.VMEM((24, 24), F32),
            pltpu.VMEM((24, 24), F32),
        ),
        in_specs=[hbm] * 9,
        out_specs=(vmem,) * 4,
        scratch_shapes=[
            *[pltpu.VMEM((states, length), F32)] * 4,
            pltpu.VMEM(tile_values.shape, BF16),
            pltpu.SMEM((slots,), jnp.int32),
            pltpu.SMEM((slots,), jnp.int32),
            pltpu.SMEM((1,), jnp.int32),
            pltpu.VMEM((states, 24), F32),
            pltpu.VMEM((1, 128), F32),
            pltpu.VMEM((cols_n, 1, 128), F32),
            pltpu.VMEM((rows_n, 1, 128), F32),
            pltpu.VMEM((1, 128), F32),
            pltpu.VMEM((rows_n, 1, 128), F32),
            pltpu.VMEM((16, 128), word),
            pltpu.VMEM((cols_n, 16, 128), word),
            pltpu.VMEM((rows_n, 16, 128), word),
            pltpu.VMEM((32, 128), word),
            pltpu.VMEM((cols_n, 32, 128), word),
            pltpu.VMEM((rows_n, 32, 128), word),
            pltpu.VMEM((4, 8, 128), F32),
            pltpu.VMEM((rows_n // near_of(rows_n), 8, 128), F32),
            pltpu.VMEM((near_of(rows_n), 8, 128), F32),
            pltpu.VMEM((near_of(cols_n), 8, 128), F32),
            pltpu.VMEM((cols_n // near_of(cols_n), 8, 128), F32),
            pltpu.VMEM((2, 128), F32),
            pltpu.VMEM((rows_n, 2, 128), F32),
            pltpu.VMEM((2, 128), F32),
            pltpu.VMEM((cols_n, 2, 128), F32),
            pltpu.VMEM((cols_n, 16, 128), BF16),
            pltpu.VMEM((rows_n, 16, 128), BF16),
            pltpu.VMEM((cols_n, 16, 128), BF16),
            pltpu.VMEM((rows_n, 16, 128), BF16),
            pltpu.SemaphoreType.DMA((9,)),
            pltpu.SemaphoreType.DMA((21,)),
            pltpu.SemaphoreType.DMA((21,)),
        ],
        compiler_params=pltpu.CompilerParams(
            collective_id=0, has_side_effects=True, vmem_limit_bytes=LIMIT
        ),
        name="step",
    )(x_block, hx_block, p_block, hp_block, tile_values, tile_rows, tile_cols, tile_count, coeffs.T)
    return finish(outs)


def solution(mesh):
    both = ("row", "col")
    return jax.shard_map(
        body,
        mesh=mesh,
        in_specs=(
            P(None, both), P(None, both), P(None, both), P(None, both),
            P(both, None, None), P(both), P(both), P(both), P(),
        ),
        out_specs=(P(), P(), P(None, both), P(None, both)),
        check_vma=False,
    )
```
